256 devices in a mesh: seq: 16 (over x, y), dp: 16 (over z, core).
Axes of the slice: x: 4, y: 4, z: 8, core: 2. Of those that a mesh axis runs over, the one named last changes fastest.
Arguments:
- query_rows: bfloat16 [16, 6144, 2048], P('dp', 'seq'), may hold values from -30 to 30
- key_rows: bfloat16 [16, 6144, 2048], P('dp', 'seq'), may hold values from -30 to 30
- value_rows: bfloat16 [16, 6144, 2048], P('dp', 'seq'), may hold values from -6 to 6
- key_tiles: int32 [16, 16, 4], P('dp'), may hold values from 0 to 15, as said below
- tile_counts: int32 [16, 16], P('dp'), may hold values from 2 to 4, as said below
- out_weight: bfloat16 [2048, 3072], P('dp'), may hold values from -0.125 to 0.125
- gate_vector: bfloat16 [16, 3072], P('dp'), may hold values from -4 to 4
Outputs:
- gated_out: bfloat16 [16, 6144, 3072], P('dp', 'seq')
The draws below stay inside these ranges and needn't reach their ends.
Inputs may be any that keep to these rules, and one draw needn't show every extreme that they name: `key_tiles`: in each row of a video the 4 entries are distinct tiles of that video; only the first tile_counts entries are used. `tile_counts`: each video has some query tile that uses all 4 slots.
All inputs are finite; a program needn't handle non-finite values.
Results may differ from the reference program's by a relative error of at most 0.007.
Values may be sent and summed in bfloat16 or wider, within the bound.
A program may use at most 128 MiB of HBM per device.

```python
import math
import jax
import jax.numpy as jnp
from jax import lax

D = 3072
HEADS = 16
HD = 128
TILE = 384
SPT = 2
MAXK = 4
INNER = 2048
VIDEOS = 16
TILES = 16
TOKENS_V = 6144


def row_field(key, low_scale, high_scale):
    key_base, key_scale = jax.random.split(key, 2)
    shape = (VIDEOS, TOKENS_V, HEADS, HD)
    draws = jnp.clip(jax.random.normal(key_base, shape, jnp.float32), -6.0, 6.0)
    row_scale = jnp.exp(jax.random.uniform(key_scale, (VIDEOS, TOKENS_V, HEADS, 1), jnp.float32, math.log(low_scale), math.log(high_scale)))
    return draws * row_scale


def draw_query_rows(key, part):
    field = row_field(jax.random.fold_in(key, 1), 0.4, 4.0)
    return field.reshape(VIDEOS, TOKENS_V, HEADS * HD).astype(jnp.bfloat16)


def draw_key_rows(key, part):
    field = row_field(jax.random.fold_in(key, 2), 0.5, 2.5)
    return field.reshape(VIDEOS, TOKENS_V, HEADS * HD).astype(jnp.bfloat16)


def draw_key_tiles(key, part):
    jitter = jax.random.randint(jax.random.fold_in(key, 3), (VIDEOS, TILES, TILES), 0, 1000)
    tile_time = jnp.arange(TILES, dtype=jnp.int32) // SPT
    time_gap = jnp.abs(tile_time[:, None] - tile_time[None, :])
    ranking = (time_gap[None, :, :] * 1000 + jitter) * TILES + jnp.arange(TILES, dtype=jnp.int32)[None, None, :]
    sorted_tiles = jnp.argsort(ranking, axis=-1, stable=True)
    return sorted_tiles[:, :, :MAXK].astype(jnp.int32)


def draw_tile_counts(key, part):
    key_count, key_full = jax.random.split(jax.random.fold_in(key, 4))
    counted = jax.random.randint(key_count, (VIDEOS, TILES), 2, MAXK + 1)
    full_tile = jax.random.randint(key_full, (VIDEOS,), 0, TILES)
    tile_index = jnp.arange(TILES, dtype=jnp.int32)
    return jnp.where(tile_index[None, :] == full_tile[:, None], MAXK, counted).astype(jnp.int32)


def levels(rng, dims, cuts, low, top_value):
    loudness = 1.0
    for axis_at, parts in cuts:
        steps = jax.random.uniform(jax.random.fold_in(jax.random.fold_in(rng, 6), axis_at), (parts,), jnp.float32, low / len(cuts), top_value / len(cuts))
        loudness = loudness * jnp.repeat(jnp.exp(steps), dims[axis_at] // parts).reshape((-1,) + (1,) * (len(dims) - 1 - axis_at))
    return loudness


def centred(stream_key, extent, scale, limit, shards=(), held_as=jnp.bfloat16):
    result = jax.random.normal(stream_key, extent, jnp.float32) * scale
    if len(shards) > 0:
        result = levels(stream_key, extent, shards, -0.22, 0.18) * result
    return jnp.clip(result, min=-limit, max=limit).astype(held_as)


def setup_inputs(seed: int = 0) -> dict:
    keys = jax.random.split(jax.random.key(seed), 8)
    return {
        "query_rows": draw_query_rows(jax.random.fold_in(keys[7], 71), 0),
        "key_rows": draw_key_rows(jax.random.fold_in(keys[7], 71), 0),
        "value_rows": centred(keys[2], (VIDEOS, TOKENS_V, INNER), 1.0, 6.0, ((0, 16), (1, 16))),
        "key_tiles": draw_key_tiles(jax.random.fold_in(keys[7], 71), 0),
        "tile_counts": draw_tile_counts(jax.random.fold_in(keys[7], 71), 0),
        "out_weight": centred(keys[5], (INNER, D), INNER ** -0.5, 0.125, ((0, 16),)),
        "gate_vector": centred(keys[6], (VIDEOS, D), 1.0, 4.0, ((0, 16),)),
    }


def attend_head(query, key_field, value_field, tile_list, tile_count):
    tile_total = query.shape[0] // TILE
    query_tiles = query.astype(jnp.float32).reshape(tile_total, TILE, HD)
    key_blocks = key_field.astype(jnp.float32).reshape(tile_total, TILE, HD)
    value_blocks = value_field.astype(jnp.float32).reshape(tile_total, TILE, HD)
    key_chosen = key_blocks[tile_list].reshape(tile_total, MAXK * TILE, HD)
    value_chosen = value_blocks[tile_list].reshape(tile_total, MAXK * TILE, HD)
    scores = jnp.einsum('atd,asd->ats', query_tiles, key_chosen) * (1.0 / math.sqrt(HD))
    slot_index = jnp.arange(MAXK * TILE, dtype=jnp.int32) // TILE
    is_live = slot_index[None, None, :] < tile_count[:, None, None]
    scores = jnp.where(is_live, scores, -jnp.inf)
    row_top = lax.optimization_barrier(jnp.max(scores, axis=-1, keepdims=True))
    weights = jnp.exp(scores - row_top)
    row_total = lax.optimization_barrier(jnp.sum(weights, axis=-1, keepdims=True))
    rounded = lax.optimization_barrier(weights.astype(jnp.bfloat16)).astype(jnp.float32)
    mixed = jnp.einsum('ats,asd->atd', rounded, value_chosen) / row_total
    return mixed.reshape(tile_total * TILE, HD).astype(jnp.bfloat16)

def reference(query_rows, key_rows, value_rows, key_tiles, tile_counts, out_weight, gate_vector):

    def one_video(operands):
        query, key_field, value_field, tile_list, tile_count, gate_row = operands

        def split_heads(field):
            return field.reshape(TOKENS_V, HEADS, HD).transpose(1, 0, 2)

        def per_head(fields):
            return attend_head(fields[0], fields[1], fields[2], tile_list, tile_count)
        heads_out = lax.map(per_head, (split_heads(query), split_heads(key_field), split_heads(value_field)))
        attended = heads_out.transpose(1, 0, 2).reshape(TOKENS_V, HEADS * HD)
        projected = jnp.dot(attended, out_weight, preferred_element_type=jnp.float32)
        return (gate_row.astype(jnp.float32)[None, :] * projected).astype(jnp.bfloat16)
    return lax.map(one_video, (query_rows, key_rows, value_rows, key_tiles, tile_counts, gate_vector))
```

```python
import math

import jax
import jax.numpy as jnp
from jax import lax
from jax.experimental import pallas as pl
from jax.experimental.pallas import tpu as pltpu
from jax.sharding import PartitionSpec as P

HD = 128
TILE = 384
MAXK = 4
SIDE = 4
RING = 8
PEERS = SIDE * SIDE - 1
D = 3072
SUBS = 2
PIECE = HD // (2 * SUBS)
NCHUNK = 512
MESH = pl.DeviceIdType.MESH
ORDER_X = (1, 3, 0, 0, 1, 3, 1, 3, 2, 2, 1, 3, 2, 2, 0, 0)
ORDER_Y = (0, 0, 1, 3, 1, 3, 3, 1, 1, 3, 2, 2, 2, 0, 2, 0)
TO_EXP2 = math.log2(math.e) / math.sqrt(HD)


def packed(digits):
    value = sum(d << (2 * i) for i, d in enumerate(digits))
    return value - (1 << 32) if value >= 1 << 31 else value


def digit(digits, i):
    if isinstance(i, int):
        return digits[i]
    return lax.shift_right_logical(jnp.int32(packed(digits)), 2 * i) & 3


def attend(query, kbuf, vbuf, key_tiles, tile_counts, a):
    count = tile_counts[a]
    scores, tops, biases = [], [], []
    for j in range(MAXK):
        s = lax.dot_general(
            query, kbuf[key_tiles[a, j]], (((1,), (1,)), ((), ())), preferred_element_type=jnp.float32
        )
        bias = jnp.where(j < count, 0.0, -jnp.inf).astype(jnp.float32)
        top = jnp.maximum(jnp.maximum(s[:, :HD], s[:, HD : 2 * HD]), s[:, 2 * HD :])
        scores.append(s)
        biases.append(bias)
        tops.append(top if j < 2 else top + bias)
    top = jnp.maximum(jnp.maximum(tops[0], tops[1]), jnp.maximum(tops[2], tops[3]))
    row_top = jnp.max(top, axis=-1, keepdims=True)
    parts, mixed = [], None
    for j in range(MAXK):
        shift = row_top if j < 2 else row_top - biases[j]
        weights = jnp.exp2((scores[j] - shift) * TO_EXP2)
        parts.append(weights[:, :HD] + weights[:, HD : 2 * HD] + weights[:, 2 * HD :])
        part = jnp.dot(
            weights.astype(jnp.bfloat16), vbuf[key_tiles[a, j]], preferred_element_type=jnp.float32
        )
        mixed = part if mixed is None else mixed + part
    total = jnp.sum((parts[0] + parts[1]) + (parts[2] + parts[3]), axis=-1, keepdims=True)
    return (mixed / total).astype(jnp.bfloat16)


def kernel(
    query_rows, key_rows, value_rows, key_tiles, tile_counts, weight, gate, out,
    kbuf, vbuf, qbuf, obuf, orecv, wbuf, acc,
    k_send, k_recv, v_send, v_recv, q_send, q_recv, o_send, o_recv, own_sem,
    w_send, w_recv, c_send, c_recv,
):
    seq, dp = lax.axis_index("seq"), lax.axis_index("dp")
    x, y, z, core = seq // SIDE, seq % SIDE, dp // 2, dp % 2
    other = z * 2 + 1 - core
    nexts = (((z + 1) % RING) * 2 + core, ((z + RING - 1) % RING) * 2 + core)

    def partner(i, sign=1):
        dx, dy = digit(ORDER_X, i), digit(ORDER_Y, i)
        return ((x + sign * dx + SIDE) % SIDE) * SIDE + (y + sign * dy + SIDE) % SIDE

    def remote(src, dst, send, recv, where):
        return pltpu.make_async_remote_copy(
            src_ref=src, dst_ref=dst, send_sem=send, recv_sem=recv, device_id=where, device_id_type=MESH
        )

    barrier = pltpu.get_barrier_semaphore()
    for i in range(PEERS):
        pl.semaphore_signal(barrier, inc=1, device_id=(partner(i), dp), device_id_type=MESH)
    for where in (*nexts, other):
        pl.semaphore_signal(barrier, inc=1, device_id=(seq, where), device_id_type=MESH)

    def head_columns(i):
        return pl.ds(pl.multiple_of(partner(i) * HD, HD), HD)

    mine = pl.ds(pl.multiple_of(seq * HD, HD), HD)
    own = [
        pltpu.make_async_copy(key_rows.at[:, mine], kbuf.at[seq], own_sem.at[0]),
        pltpu.make_async_copy(value_rows.at[:, mine], vbuf.at[seq], own_sem.at[1]),
        pltpu.make_async_copy(query_rows.at[:, mine], qbuf.at[PEERS], own_sem.at[2]),
        pltpu.make_async_copy(weight, wbuf.at[dp], own_sem.at[3]),
    ]
    for copy in own:
        copy.start()
    pl.semaphore_wait(barrier, PEERS + 3)

    def piece(p):
        return pl.ds(p * PIECE, PIECE)

    def hop(p, t, block, src=None):
        place = wbuf.at[block, piece(p)]
        return remote(place if src is None else src, place, w_send.at[p, t], w_recv.at[p, t], (seq, nexts[p // SUBS]))

    def swap(p, t, block, src=None):
        place = wbuf.at[block, piece(p)]
        return remote(place if src is None else src, place, c_send.at[p, t], c_recv.at[p, t], (seq, other))

    def block_of(p, t, which):
        return ((z - t + RING) % RING if p < SUBS else (z + t) % RING) * 2 + which

    for p in range(2 * SUBS):
        hop(p, 0, dp, weight.at[piece(p)]).start()

    for i in range(PEERS):
        remote(key_rows.at[:, head_columns(i)], kbuf.at[seq], k_send, k_recv, (partner(i), dp)).start()
    for i in range(PEERS):
        remote(value_rows.at[:, head_columns(i)], vbuf.at[seq], v_send, v_recv, (partner(i), dp)).start()
    for i in range(PEERS):
        remote(query_rows.at[:, head_columns(i)], qbuf.at[i], q_send, q_recv.at[i], (partner(i), dp)).start()
    for p in range(2 * SUBS):
        swap(p, 0, dp, weight.at[piece(p)]).start()

    def tick(t, sub):
        for p in (sub, SUBS + sub):
            block = block_of(p, t, core)
            hop(p, t - 1, block).wait_recv()

            @pl.when(t < RING - 1)
            def _():
                hop(p, t, block).start()

            swap(p, t, block).start()

    for t in (1, 2, 3):
        for sub in range(SUBS):
            tick(t, sub)
    all_but_one = pl.ds(0, PEERS)
    for copy in own:
        copy.wait()
    pltpu.make_async_copy(kbuf.at[all_but_one], kbuf.at[all_but_one], k_recv).wait()
    pltpu.make_async_copy(vbuf.at[all_but_one], vbuf.at[all_but_one], v_recv).wait()

    orecv[PEERS] = attend(qbuf[PEERS], kbuf, vbuf, key_tiles, tile_counts, seq)

    def answer(i):
        a = partner(i, -1)
        return remote(obuf.at[i], orecv.at[i], o_send.at[i], o_recv.at[i], (a, dp))

    def step(i, carry):
        a = partner(i, -1)

        @pl.when(i % 2 == 0)
        def _():
            u = i // 2
            for sub in range(SUBS):

                @pl.when(u % 2 == sub)
                def _():
                    tick(4 + u // 2, sub)

        pltpu.make_async_copy(qbuf.at[i], qbuf.at[i], q_recv.at[i]).wait()
        obuf[i] = attend(qbuf[i], kbuf, vbuf, key_tiles, tile_counts, a)
        answer(i).start()
        return carry

    lax.fori_loop(0, PEERS, step, 0)

    for p in range(2 * SUBS):
        for t in range(RING):
            swap(p, t, block_of(p, t, 1 - core)).wait_recv()

    group = 4
    for g in range(0, PEERS + 1, group):
        for i in range(g, min(g + group, PEERS)):
            pltpu.make_async_copy(orecv.at[i], orecv.at[i], o_recv.at[i]).wait()
        rows = jnp.concatenate([orecv[i] for i in range(g, g + group)], axis=1)

        def project(n, carry):
            at = pl.ds(pl.multiple_of(n * NCHUNK, NCHUNK), NCHUNK)
            block = jnp.concatenate([wbuf[partner(i), :, at] for i in range(g, g + group)], axis=0)
            product = jnp.dot(rows, block, preferred_element_type=jnp.float32)
            if g > 0:
                product = acc[:, at] + product
            if g + group <= PEERS:
                acc[:, at] = product
            else:
                out[:, at] = (gate[:, at].astype(jnp.float32) * product).astype(jnp.bfloat16)
            return carry

        lax.fori_loop(0, D // NCHUNK, project, 0)

    pltpu.make_async_copy(kbuf.at[all_but_one], kbuf.at[all_but_one], k_send).wait()
    pltpu.make_async_copy(vbuf.at[all_but_one], vbuf.at[all_but_one], v_send).wait()
    pltpu.make_async_copy(qbuf.at[all_but_one], qbuf.at[all_but_one], q_send).wait()
    for i in range(PEERS):
        answer(i).wait_send()
    for p in range(2 * SUBS):
        for t in range(RING):
            swap(p, t, dp).wait_send()
            if t < RING - 1:
                hop(p, t, dp).wait_send()


def shards(query_rows, key_rows, value_rows, key_tiles, tile_counts, out_weight, gate_vector):
    dma = pltpu.SemaphoreType.DMA
    far = pl.BlockSpec(memory_space=pltpu.HBM)
    near = pl.BlockSpec(memory_space=pltpu.VMEM)
    scalars = pl.BlockSpec(memory_space=pltpu.SMEM)
    tiles = PEERS + 1
    blocks = RING * 2
    result = pl.pallas_call(
        kernel,
        name="attention_and_projection",
        out_shape=jax.ShapeDtypeStruct((TILE, D), jnp.bfloat16),
        in_specs=[far, far, far, scalars, scalars, far, near],
        out_specs=near,
        scratch_shapes=[
            pltpu.VMEM((tiles, TILE, HD), jnp.bfloat16),
            pltpu.VMEM((tiles, TILE, HD), jnp.bfloat16),
            pltpu.VMEM((tiles, TILE, HD), jnp.bfloat16),
            pltpu.VMEM((tiles, TILE, HD), jnp.bfloat16),
            pltpu.VMEM((tiles, TILE, HD), jnp.bfloat16),
            pltpu.VMEM((blocks, HD, D), jnp.bfloat16),
            pltpu.VMEM((TILE, D), jnp.float32),
            dma, dma, dma, dma, dma, dma((tiles,)), dma((tiles,)), dma((tiles,)), dma((4,)),
            dma((2 * SUBS, RING)), dma((2 * SUBS, RING)), dma((2 * SUBS, RING)), dma((2 * SUBS, RING)),
        ],
        compiler_params=pltpu.CompilerParams(
            collective_id=0, has_side_effects=True, vmem_limit_bytes=60 << 20
        ),
        cost_estimate=pl.CostEstimate(
            flops=10_000_000_000, bytes_accessed=10_000_000, transcendentals=9_000_000
        ),
    )(query_rows[0], key_rows[0], value_rows[0], key_tiles[0], tile_counts[0], out_weight, gate_vector)
    return result[None]


def solution(mesh):
    in_specs = (
        P("dp", "seq", None),
        P("dp", "seq", None),
        P("dp", "seq", None),
        P("dp", None, None),
        P("dp", None),
        P("dp", None),
        P("dp", None),
    )
    out_specs = P("dp", "seq", None)
    return jax.shard_map(shards, mesh=mesh, in_specs=in_specs, out_specs=out_specs, check_vma=False)
```

```python
import math

import jax
import jax.numpy as jnp
from jax import lax
from jax.experimental import pallas as pl
from jax.experimental.pallas import tpu as pltpu
from jax.sharding import PartitionSpec as P

HD = 128
TILE = 384
MAXK = 4
SIDE = 4
RING = 8
PEERS = SIDE * SIDE - 1
D = 3072
PIECES = 4
PIECE = HD // PIECES
AWAY = RING // 2 - 1
COMING = AWAY * PIECES + PIECES // 2
EARLY = 7
NCHUNK = 512
LAST = 2
MESH = pl.DeviceIdType.MESH
ORDER_X = (1, 3, 0, 0, 1, 3, 1, 3, 2, 2, 1, 3, 2, 2, 0, 0)
ORDER_Y = (0, 0, 1, 3, 1, 3, 3, 1, 1, 3, 2, 2, 2, 0, 2, 0)
TO_EXP2 = math.log2(math.e) / math.sqrt(HD)


def packed(digits):
    value = sum(d << (2 * i) for i, d in enumerate(digits))
    return value - (1 << 32) if value >= 1 << 31 else value


def digit(digits, i):
    if isinstance(i, int):
        return digits[i]
    return lax.shift_right_logical(jnp.int32(packed(digits)), 2 * i) & 3


def turn(n):
    if isinstance(n, int):
        return LAST if n == PEERS - 1 else n + (n >= LAST)
    return jnp.where(n == PEERS - 1, LAST, jnp.where(n < LAST, n, n + 1))


def attend(query, kbuf, vbuf, key_tiles, tile_counts, a):
    count = tile_counts[a]
    scores, tops, biases = [], [], []
    for j in range(MAXK):
        s = lax.dot_general(
            query, kbuf[key_tiles[j, a]], (((1,), (1,)), ((), ())), preferred_element_type=jnp.float32
        )
        bias = jnp.where(j < count, 0.0, -jnp.inf).astype(jnp.float32)
        top = jnp.maximum(jnp.maximum(s[:, :HD], s[:, HD : 2 * HD]), s[:, 2 * HD :])
        scores.append(s)
        biases.append(bias)
        tops.append(top if j < 2 else top + bias)
    top = jnp.maximum(jnp.maximum(tops[0], tops[1]), jnp.maximum(tops[2], tops[3]))
    row_top = jnp.max(top, axis=-1, keepdims=True)
    parts, mixed = [], None
    for j in range(MAXK):
        shift = row_top if j < 2 else row_top - biases[j]
        weights = jnp.exp2((scores[j] - shift) * TO_EXP2)
        parts.append(weights[:, :HD] + weights[:, HD : 2 * HD] + weights[:, 2 * HD :])
        part = jnp.dot(
            weights.astype(jnp.bfloat16), vbuf[key_tiles[j, a]], preferred_element_type=jnp.float32
        )
        mixed = part if mixed is None else mixed + part
    total = jnp.sum((parts[0] + parts[1]) + (parts[2] + parts[3]), axis=-1, keepdims=True)
    return (mixed / total).astype(jnp.bfloat16)


def kernel(
    query_rows, key_rows, value_rows, key_tiles, tile_counts, weight, gate, out,
    kbuf, vbuf, qbuf, obuf, orecv, wbuf, acc,
    k_send, k_recv, v_send, v_recv, q_send, q_recv, o_send, o_recv, own_sem,
    w_send, w_recv, c_send, c_recv,
):
    seq, dp = lax.axis_index("seq"), lax.axis_index("dp")
    x, y, z, core = seq // SIDE, seq % SIDE, dp // 2, dp % 2
    other = z * 2 + 1 - core
    nexts = (((z + 1) % RING) * 2 + core, ((z + RING - 1) % RING) * 2 + core)

    def partner(i, sign=1):
        dx, dy = digit(ORDER_X, i), digit(ORDER_Y, i)
        return ((x + sign * dx + SIDE) % SIDE) * SIDE + (y + sign * dy + SIDE) % SIDE

    def remote(src, dst, send, recv, where):
        return pltpu.make_async_remote_copy(
            src_ref=src, dst_ref=dst, send_sem=send, recv_sem=recv, device_id=where, device_id_type=MESH
        )

    def bytes_of(buffer, count, semaphore):
        part = buffer.at[pl.ds(0, count)]
        return pltpu.make_async_copy(part, part, semaphore)

    barrier = pltpu.get_barrier_semaphore()
    for i in range(PEERS):
        pl.semaphore_signal(barrier, inc=1, device_id=(partner(i), dp), device_id_type=MESH)
    for where in (*nexts, other):
        pl.semaphore_signal(barrier, inc=1, device_id=(seq, where), device_id_type=MESH)

    def head_columns(i):
        return pl.ds(pl.multiple_of(partner(i) * HD, HD), HD)

    mine = pl.ds(pl.multiple_of(seq * HD, HD), HD)
    own = [
        pltpu.make_async_copy(key_rows.at[:, mine], kbuf.at[seq], own_sem),
        pltpu.make_async_copy(value_rows.at[:, mine], vbuf.at[seq], own_sem),
        pltpu.make_async_copy(query_rows.at[:, mine], qbuf.at[PEERS], own_sem),
        pltpu.make_async_copy(weight, wbuf.at[dp], own_sem),
    ]
    for copy in own:
        copy.start()
    pl.semaphore_wait(barrier, PEERS + 3)

    def piece(p):
        return pl.ds(pl.multiple_of(p * PIECE, PIECE), PIECE)

    def hop(way, n, p, block, src=None):
        place = wbuf.at[block, piece(p)]
        return remote(place if src is None else src, place, w_send, w_recv.at[way, n], (seq, nexts[way]))

    for p in range(PIECES):
        for way in range(2):
            hop(way, p, p, dp, weight.at[piece(p)]).start()

    for i in range(PEERS):
        remote(key_rows.at[:, head_columns(i)], kbuf.at[seq], k_send, k_recv, (partner(i), dp)).start()
    for i in range(PEERS):
        remote(value_rows.at[:, head_columns(i)], vbuf.at[seq], v_send, v_recv, (partner(i), dp)).start()
    for i in range(PEERS):
        remote(query_rows.at[:, head_columns(i)], qbuf.at[i], q_send, q_recv.at[i], (partner(i), dp)).start()
    remote(weight, wbuf.at[dp], c_send, c_recv, (seq, other)).start()

    def tick(n):
        q = n % PIECES
        for way in range(2):
            p = q + way * (PIECES // 2) * (n // (AWAY * PIECES))
            far = n // PIECES + 1
            block = ((z + RING - far) % RING if way == 0 else (z + far) % RING) * 2 + core
            hop(way, n, p, block).wait_recv()

            @pl.when((n < (AWAY - 1) * PIECES) | ((n < AWAY * PIECES) & (q // (PIECES // 2) == way)))
            def _():
                last = AWAY * PIECES + q % (PIECES // 2)
                hop(way, jnp.where(n < (AWAY - 1) * PIECES, n + PIECES, last), p, block).start()

            place = wbuf.at[block, piece(p)]
            remote(place, place, c_send, c_recv, (seq, other)).start()

    for n in range(EARLY):
        tick(n)
    bytes_of(kbuf, len(own) - 1 + HD * D // (TILE * HD), own_sem).wait()
    bytes_of(kbuf, PEERS, k_recv).wait()
    bytes_of(vbuf, PEERS, v_recv).wait()

    orecv[PEERS] = attend(qbuf[PEERS], kbuf, vbuf, key_tiles, tile_counts, seq)

    def answer(i):
        a = partner(i, -1)
        return remote(obuf.at[i], orecv.at[i], o_send, o_recv.at[i], (a, dp))

    def step(n, carry):
        i = turn(n)
        a = partner(i, -1)

        @pl.when(n % 3 == 1)
        def _():
            tick(EARLY + n // 3)

        pltpu.make_async_copy(qbuf.at[i], qbuf.at[i], q_recv.at[i]).wait()
        obuf[i] = attend(qbuf[i], kbuf, vbuf, key_tiles, tile_counts, a)
        answer(i).start()
        return carry

    lax.fori_loop(0, PEERS, step, 0)
    for n in range(EARLY + PEERS // 3, COMING):
        tick(n)
    bytes_of(wbuf, RING, c_recv).wait()

    order = [PEERS, *(turn(n) for n in range(PEERS))]
    done = 0
    for group in (4, 4, 4, 2, 2):
        these = order[done : done + group]
        done += group
        for i in these:
            if i < PEERS:
                pltpu.make_async_copy(orecv.at[i], orecv.at[i], o_recv.at[i]).wait()
        rows = jnp.concatenate([orecv[i] for i in these], axis=1)
        for n in range(0, D, NCHUNK):
            at = pl.ds(n, NCHUNK)
            block = jnp.concatenate([wbuf[partner(i), :, at] for i in these], axis=0)
            product = jnp.dot(rows, block, preferred_element_type=jnp.float32)
            if done > group:
                product = acc[:, at] + product
            if done <= PEERS:
                acc[:, at] = product
            else:
                out[:, at] = (gate[:, at].astype(jnp.float32) * product).astype(jnp.bfloat16)

    bytes_of(kbuf, PEERS, k_send).wait()
    bytes_of(vbuf, PEERS, v_send).wait()
    bytes_of(qbuf, PEERS, q_send).wait()
    bytes_of(obuf, PEERS, o_send).wait()
    bytes_of(wbuf, RING - 1, w_send).wait()
    bytes_of(wbuf, RING, c_send).wait()


def shards(query_rows, key_rows, value_rows, key_tiles, tile_counts, out_weight, gate_vector):
    dma = pltpu.SemaphoreType.DMA
    far = pl.BlockSpec(memory_space=pltpu.HBM)
    near = pl.BlockSpec(memory_space=pltpu.VMEM)
    scalars = pl.BlockSpec(memory_space=pltpu.SMEM)
    tiles = PEERS + 1
    blocks = RING * 2
    result = pl.pallas_call(
        kernel,
        name="attention_and_projection",
        out_shape=pltpu.VMEM((TILE, D), jnp.bfloat16),
        in_specs=[far, far, far, scalars, scalars, far, near],
        out_specs=near,
        scratch_shapes=[
            pltpu.VMEM((tiles, TILE, HD), jnp.bfloat16),
            pltpu.VMEM((tiles, TILE, HD), jnp.bfloat16),
            pltpu.VMEM((tiles, TILE, HD), jnp.bfloat16),
            pltpu.VMEM((tiles, TILE, HD), jnp.bfloat16),
            pltpu.VMEM((tiles, TILE, HD), jnp.bfloat16),
            pltpu.VMEM((blocks, HD, D), jnp.bfloat16),
            pltpu.VMEM((TILE, D), jnp.float32),
            dma, dma, dma, dma, dma, dma((PEERS,)), dma, dma((PEERS,)), dma,
            dma, dma((2, COMING)), dma, dma,
        ],
        compiler_params=pltpu.CompilerParams(
            collective_id=0, has_side_effects=True, vmem_limit_bytes=60 << 20
        ),
        cost_estimate=pl.CostEstimate(
            flops=10_000_000_000, bytes_accessed=10_000_000, transcendentals=9_000_000
        ),
    )(query_rows[0], key_rows[0], value_rows[0], key_tiles[0].T, tile_counts[0], out_weight, gate_vector)
    return result[None]


def solution(mesh):
    in_specs = (
        P("dp", "seq", None),
        P("dp", "seq", None),
        P("dp", "seq", None),
        P("dp", None, None),
        P("dp", None),
        P("dp", None),
        P("dp", None),
    )
    out_specs = P("dp", "seq", None)
    return jax.shard_map(shards, mesh=mesh, in_specs=in_specs, out_specs=out_specs, check_vma=False)
```

```python
import math

import jax
import jax.numpy as jnp
from jax import lax
from jax.experimental import pallas as pl
from jax.experimental.pallas import tpu as pltpu
from jax.sharding import PartitionSpec as P

HD = 128
TILE = 384
MAXK = 4
SIDE = 4
RING = 8
PEERS = SIDE * SIDE - 1
D = 3072
PIECES = 4
PIECE = HD // PIECES
AWAY = RING // 2 - 1
COMING = AWAY * PIECES + PIECES // 2
EARLY = 7
NCHUNK = 512
QUERY_TURNS = (0, 1, 3, 4, 5, 6, 7, 8, 9, 2, 10, 14, 11, 12, 13)
MESH = pl.DeviceIdType.MESH
ORDER_X = (1, 3, 0, 0, 1, 3, 1, 3, 2, 2, 1, 3, 2, 2, 0, 0)
ORDER_Y = (0, 0, 1, 3, 1, 3, 3, 1, 1, 3, 2, 2, 2, 0, 2, 0)
TO_EXP2 = math.log2(math.e) / math.sqrt(HD)


def packed(digits, bits):
    value = sum(d << (bits * i) for i, d in enumerate(digits))
    return jnp.int32(value - (1 << 32) if value >= 1 << 31 else value)


def digit(digits, i):
    if isinstance(i, int):
        return digits[i]
    return lax.shift_right_logical(packed(digits, 2), 2 * i) & 3


def entry(values, i):
    if isinstance(i, int):
        return values[i]
    half = packed(values[:8], 4), packed(values[8:], 4)
    return lax.shift_right_logical(jnp.where(i < 8, *half), 4 * (i % 8)) & 15


TURNS = (PEERS, *QUERY_TURNS)
TURN_X = tuple(ORDER_X[i] for i in TURNS)
TURN_Y = tuple(ORDER_Y[i] for i in TURNS)
PLACES = tuple(tuple(zip(TURN_X, TURN_Y)).index((d // SIDE, d % SIDE)) for d in range(SIDE * SIDE))


def attend(query, kbuf, vbuf, key_tiles, tile_counts, a):
    count = tile_counts[a]
    scores, tops, biases = [], [], []
    for j in range(MAXK):
        s = lax.dot_general(
            query, kbuf[key_tiles[j, a]], (((1,), (1,)), ((), ())), preferred_element_type=jnp.float32
        )
        bias = jnp.where(j < count, 0.0, -jnp.inf).astype(jnp.float32)
        top = jnp.maximum(jnp.maximum(s[:, :HD], s[:, HD : 2 * HD]), s[:, 2 * HD :])
        scores.append(s)
        biases.append(bias)
        tops.append(top if j < 2 else top + bias)
    top = jnp.maximum(jnp.maximum(tops[0], tops[1]), jnp.maximum(tops[2], tops[3]))
    row_top = jnp.max(top, axis=-1, keepdims=True)
    parts, mixed = [], None
    for j in range(MAXK):
        shift = row_top if j < 2 else row_top - biases[j]
        weights = jnp.exp2((scores[j] - shift) * TO_EXP2)
        parts.append(weights[:, :HD] + weights[:, HD : 2 * HD] + weights[:, 2 * HD :])
        part = jnp.dot(
            weights.astype(jnp.bfloat16), vbuf[key_tiles[j, a]], preferred_element_type=jnp.float32
        )
        mixed = part if mixed is None else mixed + part
    total = jnp.sum((parts[0] + parts[1]) + (parts[2] + parts[3]), axis=-1, keepdims=True)
    return (mixed / total).astype(jnp.bfloat16)


def kernel(
    query_rows, key_rows, value_rows, key_tiles, tile_counts, weight, gate, out,
    kbuf, vbuf, qbuf, obuf, orecv, wbuf, acc,
    k_send, k_recv, v_send, v_recv, q_send, q_recv, o_send, o_recv, own_sem,
    w_send, w_recv, c_send, c_recv, c_far, ready,
):
    seq, dp = lax.axis_index("seq"), lax.axis_index("dp")
    x, y, z, core = seq // SIDE, seq % SIDE, dp // 2, dp % 2
    other = z * 2 + 1 - core
    nexts = (((z + 1) % RING) * 2 + core, ((z + RING - 1) % RING) * 2 + core)

    def partner(i, sign=1):
        dx, dy = digit(ORDER_X, i), digit(ORDER_Y, i)
        return ((x + sign * dx + SIDE) % SIDE) * SIDE + (y + sign * dy + SIDE) % SIDE

    def remote(src, dst, send, recv, where):
        return pltpu.make_async_remote_copy(
            src_ref=src, dst_ref=dst, send_sem=send, recv_sem=recv, device_id=where, device_id_type=MESH
        )

    def bytes_of(buffer, count, semaphore):
        part = buffer.at[pl.ds(0, count)]
        return pltpu.make_async_copy(part, part, semaphore)

    barrier = pltpu.get_barrier_semaphore()
    for i in range(PEERS):
        pl.semaphore_signal(barrier, inc=1, device_id=(partner(i), dp), device_id_type=MESH)
    pl.semaphore_signal(barrier, inc=1, device_id=(seq, other), device_id_type=MESH)

    @pl.when(z % 2 == 0)
    def _():
        for where in nexts:
            pl.semaphore_signal(barrier, inc=1, device_id=(seq, where), device_id_type=MESH)

    def head_columns(i):
        return pl.ds(pl.multiple_of(partner(i) * HD, HD), HD)

    mine = pl.ds(pl.multiple_of(seq * HD, HD), HD)
    own = [
        pltpu.make_async_copy(key_rows.at[:, mine], kbuf.at[seq], own_sem),
        pltpu.make_async_copy(value_rows.at[:, mine], vbuf.at[seq], own_sem),
        pltpu.make_async_copy(query_rows.at[:, mine], qbuf.at[PEERS], own_sem),
        pltpu.make_async_copy(weight, wbuf.at[dp], own_sem),
    ]
    for copy in own:
        copy.start()
    pl.semaphore_wait(barrier, PEERS + 1 + 2 * (z % 2))

    @pl.when(z % 2 == 1)
    def _():
        for where in nexts:
            pl.semaphore_signal(ready, inc=1, device_id=(seq, where), device_id_type=MESH)


    def piece(p):
        return pl.ds(pl.multiple_of(p * PIECE, PIECE), PIECE)

    def hop(way, n, p, block, src=None):
        place = wbuf.at[block, piece(p)]
        return remote(place if src is None else src, place, w_send, w_recv.at[way, n], (seq, nexts[way]))

    for i in range(PEERS):
        remote(key_rows.at[:, head_columns(i)], kbuf.at[seq], k_send, k_recv, (partner(i), dp)).start()
    for i in range(PEERS):
        remote(value_rows.at[:, head_columns(i)], vbuf.at[seq], v_send, v_recv, (partner(i), dp)).start()
    for i in range(PEERS):
        remote(query_rows.at[:, head_columns(i)], qbuf.at[i], q_send, q_recv.at[i], (partner(i), dp)).start()
    remote(weight, wbuf.at[dp], c_send, c_recv, (seq, other)).start()

    @pl.when(z % 2 == 0)
    def _():
        pl.semaphore_wait(ready, 2)

    for p in range(PIECES):
        for way in range(2):
            hop(way, p, p, dp, weight.at[piece(p)]).start()

    def tick(n, swapped):
        q = n % PIECES
        for way in range(2):
            p = q + way * (PIECES // 2) * (n // (AWAY * PIECES))
            far = n // PIECES + 1
            block = ((z + RING - far) % RING if way == 0 else (z + far) % RING) * 2 + core
            hop(way, n, p, block).wait_recv()

            @pl.when((n < (AWAY - 1) * PIECES) | ((n < AWAY * PIECES) & (q // (PIECES // 2) == way)))
            def _():
                last = AWAY * PIECES + q % (PIECES // 2)
                hop(way, jnp.where(n < (AWAY - 1) * PIECES, n + PIECES, last), p, block).start()

            place = wbuf.at[block, piece(p)]
            remote(place, place, c_send, swapped, (seq, other)).start()

    for n in range(EARLY):
        tick(n, c_recv)
    bytes_of(kbuf, len(own) - 1 + HD * D // (TILE * HD), own_sem).wait()
    bytes_of(kbuf, PEERS, k_recv).wait()
    bytes_of(vbuf, PEERS, v_recv).wait()

    orecv[seq] = attend(qbuf[PEERS], kbuf, vbuf, key_tiles, tile_counts, seq)

    def answer(i):
        a = partner(i, -1)
        return remote(obuf.at[i], orecv.at[seq], o_send, o_recv.at[seq], (a, dp))

    def step(n, carry):
        i = entry(QUERY_TURNS, n)
        a = partner(i, -1)

        @pl.when(n % 3 == 1)
        def _():
            tick(EARLY + n // 3, c_recv)

        pltpu.make_async_copy(qbuf.at[i], qbuf.at[i], q_recv.at[i]).wait()
        obuf[i] = attend(qbuf[i], kbuf, vbuf, key_tiles, tile_counts, a)
        answer(i).start()
        return carry

    lax.fori_loop(0, PEERS, step, 0)
    far = (z + RING // 2) % RING * 2
    at_a = entry(PLACES, (far // SIDE - x + SIDE) % SIDE * SIDE + (far % SIDE - y + SIDE) % SIDE)
    at_b = entry(PLACES, ((far + 1) // SIDE - x + SIDE) % SIDE * SIDE + ((far + 1) % SIDE - y + SIDE) % SIDE)
    low, high = jnp.minimum(at_a, at_b), jnp.maximum(at_a, at_b)

    def near_head(k):
        k = k + jnp.where(k >= low, 1, 0)
        k = k + jnp.where(k >= high, 1, 0)
        return (x + digit(TURN_X, k)) % SIDE * SIDE + (y + digit(TURN_Y, k)) % SIDE

    def project(heads, first=False, last=False):
        for h in heads:

            @pl.when(h != seq)
            def _():
                pltpu.make_async_copy(orecv.at[h], orecv.at[h], o_recv.at[h]).wait()

        rows = jnp.concatenate([orecv[h] for h in heads], axis=1)
        for n in range(0, D, NCHUNK):
            at = pl.ds(n, NCHUNK)
            block = jnp.concatenate([wbuf[h, :, at] for h in heads], axis=0)
            product = jnp.dot(rows, block, preferred_element_type=jnp.float32)
            if not first:
                product = acc[:, at] + product
            if last:
                out[:, at] = (gate[:, at].astype(jnp.float32) * product).astype(jnp.bfloat16)
            else:
                acc[:, at] = product

    bytes_of(wbuf, RING - 1, c_recv).wait()
    project([near_head(k) for k in range(4)], first=True)
    tick(COMING - 2, c_far)
    tick(COMING - 1, c_far)
    project([near_head(k) for k in range(4, 8)])
    bytes_of(wbuf, 1, c_far).wait()
    project([far, far + 1])
    project([near_head(k) for k in range(8, 12)])
    project([near_head(k) for k in range(12, 14)], last=True)

    bytes_of(kbuf, PEERS, k_send).wait()
    bytes_of(vbuf, PEERS, v_send).wait()
    bytes_of(qbuf, PEERS, q_send).wait()
    bytes_of(obuf, PEERS, o_send).wait()
    bytes_of(wbuf, RING - 1, w_send).wait()
    bytes_of(wbuf, RING, c_send).wait()


def shards(query_rows, key_rows, value_rows, key_tiles, tile_counts, out_weight, gate_vector):
    dma = pltpu.SemaphoreType.DMA
    far = pl.BlockSpec(memory_space=pltpu.HBM)
    near = pl.BlockSpec(memory_space=pltpu.VMEM)
    scalars = pl.BlockSpec(memory_space=pltpu.SMEM)
    tiles = PEERS + 1
    blocks = RING * 2
    result = pl.pallas_call(
        kernel,
        name="attention_and_projection",
        out_shape=pltpu.VMEM((TILE, D), jnp.bfloat16),
        in_specs=[far, far, far, scalars, scalars, far, near],
        out_specs=near,
        scratch_shapes=[
            pltpu.VMEM((tiles, TILE, HD), jnp.bfloat16),
            pltpu.VMEM((tiles, TILE, HD), jnp.bfloat16),
            pltpu.VMEM((tiles, TILE, HD), jnp.bfloat16),
            pltpu.VMEM((tiles, TILE, HD), jnp.bfloat16),
            pltpu.VMEM((tiles, TILE, HD), jnp.bfloat16),
            pltpu.VMEM((blocks, HD, D), jnp.bfloat16),
            pltpu.VMEM((TILE, D), jnp.float32),
            dma, dma, dma, dma, dma, dma((PEERS,)), dma, dma((tiles,)), dma,
            dma, dma((2, COMING)), dma, dma, dma, pltpu.SemaphoreType.REGULAR,
        ],
        compiler_params=pltpu.CompilerParams(
            collective_id=0, has_side_effects=True, vmem_limit_bytes=60 << 20
        ),
        cost_estimate=pl.CostEstimate(
            flops=10_000_000_000, bytes_accessed=10_000_000, transcendentals=9_000_000
        ),
    )(query_rows[0], key_rows[0], value_rows[0], key_tiles[0].T, tile_counts[0], out_weight, gate_vector)
    return result[None]


def solution(mesh):
    in_specs = (
        P("dp", "seq", None),
        P("dp", "seq", None),
        P("dp", "seq", None),
        P("dp", None, None),
        P("dp", None),
        P("dp", None),
        P("dp", None),
    )
    out_specs = P("dp", "seq", None)
    return jax.shard_map(shards, mesh=mesh, in_specs=in_specs, out_specs=out_specs, check_vma=False)
```

```python
import math

import jax
import jax.numpy as jnp
from jax import lax
from jax.experimental import pallas as pl
from jax.experimental.pallas import tpu as pltpu
from jax.sharding import PartitionSpec as P

HD = 128
TILE = 384
MAXK = 4
SIDE = 4
RING = 8
PEERS = SIDE * SIDE - 1
D = 3072
PIECES = 4
PIECE = HD // PIECES
AWAY = RING // 2 - 1
COMING = AWAY * PIECES + PIECES // 2
EARLY = 7
NCHUNK = 512
QUERY_TURNS = (0, 1, 3, 4, 5, 6, 7, 8, 9, 2, 10, 14, 11, 12, 13)
MESH = pl.DeviceIdType.MESH
ORDER_X = (1, 3, 0, 0, 1, 3, 1, 3, 2, 2, 1, 3, 2, 2, 0, 0)
ORDER_Y = (0, 0, 1, 3, 1, 3, 3, 1, 1, 3, 2, 2, 2, 0, 2, 0)
TO_EXP2 = math.log2(math.e) / math.sqrt(HD)


def packed(digits, bits):
    value = sum(d << (bits * i) for i, d in enumerate(digits))
    return jnp.int32(value - (1 << 32) if value >= 1 << 31 else value)


def digit(digits, i):
    if isinstance(i, int):
        return digits[i]
    return lax.shift_right_logical(packed(digits, 2), 2 * i) & 3


def entry(values, i):
    if isinstance(i, int):
        return values[i]
    half = packed(values[:8], 4), packed(values[8:], 4)
    return lax.shift_right_logical(jnp.where(i < 8, *half), 4 * (i % 8)) & 15


TURNS = (PEERS, *QUERY_TURNS)
TURN_X = tuple(ORDER_X[i] for i in TURNS)
TURN_Y = tuple(ORDER_Y[i] for i in TURNS)
PLACES = tuple(tuple(zip(TURN_X, TURN_Y)).index((d // SIDE, d % SIDE)) for d in range(SIDE * SIDE))


def attend(query, kbuf, vbuf, key_tiles, tile_counts, a):
    count = tile_counts[a]
    scores, tops, biases = [], [], []
    for j in range(MAXK):
        s = lax.dot_general(
            query, kbuf[key_tiles[j, a]], (((1,), (1,)), ((), ())), preferred_element_type=jnp.float32
        )
        bias = jnp.where(j < count, 0.0, -jnp.inf).astype(jnp.float32)
        top = jnp.maximum(jnp.maximum(s[:, :HD], s[:, HD : 2 * HD]), s[:, 2 * HD :])
        scores.append(s)
        biases.append(bias)
        tops.append(top if j < 2 else top + bias)
    top = jnp.maximum(jnp.maximum(tops[0], tops[1]), jnp.maximum(tops[2], tops[3]))
    row_top = jnp.max(top, axis=-1, keepdims=True)
    parts, mixed = [], None
    for j in range(MAXK):
        shift = row_top if j < 2 else row_top - biases[j]
        weights = jnp.exp2((scores[j] - shift) * TO_EXP2)
        parts.append(weights[:, :HD] + weights[:, HD : 2 * HD] + weights[:, 2 * HD :])
        part = jnp.dot(
            weights.astype(jnp.bfloat16), vbuf[key_tiles[j, a]], preferred_element_type=jnp.float32
        )
        mixed = part if mixed is None else mixed + part
    total = jnp.sum((parts[0] + parts[1]) + (parts[2] + parts[3]), axis=-1, keepdims=True)
    return (mixed / total).astype(jnp.bfloat16)


def kernel(
    query_rows, key_rows, value_rows, key_tiles_far, tile_counts_far, weight, gate_far, out,
    key_tiles, tile_counts, gate, kbuf, vbuf, qbuf, obuf, orecv, wbuf, acc,
    k_send, k_recv, v_send, v_recv, q_send, q_recv, o_send, o_recv, own_sem, list_sem,
    w_send, w_recv, c_send, c_recv, c_far, ready,
):
    seq, dp = lax.axis_index("seq"), lax.axis_index("dp")
    x, y, z, core = seq // SIDE, seq % SIDE, dp // 2, dp % 2
    other = z * 2 + 1 - core
    nexts = (((z + 1) % RING) * 2 + core, ((z + RING - 1) % RING) * 2 + core)

    def partner(i, sign=1):
        dx, dy = digit(ORDER_X, i), digit(ORDER_Y, i)
        return ((x + sign * dx + SIDE) % SIDE) * SIDE + (y + sign * dy + SIDE) % SIDE

    def remote(src, dst, send, recv, where):
        return pltpu.make_async_remote_copy(
            src_ref=src, dst_ref=dst, send_sem=send, recv_sem=recv, device_id=where, device_id_type=MESH
        )

    def bytes_of(buffer, count, semaphore):
        part = buffer.at[pl.ds(0, count)]
        return pltpu.make_async_copy(part, part, semaphore)

    barrier = pltpu.get_barrier_semaphore()
    for i in range(PEERS):
        pl.semaphore_signal(barrier, inc=1, device_id=(partner(i), dp), device_id_type=MESH)
    pl.semaphore_signal(barrier, inc=1, device_id=(seq, other), device_id_type=MESH)

    @pl.when(z % 2 == 0)
    def _():
        for where in nexts:
            pl.semaphore_signal(barrier, inc=1, device_id=(seq, where), device_id_type=MESH)

    def head_columns(i):
        return pl.ds(pl.multiple_of(partner(i) * HD, HD), HD)

    mine = pl.ds(pl.multiple_of(seq * HD, HD), HD)
    own = [
        pltpu.make_async_copy(key_rows.at[:, mine], kbuf.at[seq], own_sem),
        pltpu.make_async_copy(value_rows.at[:, mine], vbuf.at[seq], own_sem),
        pltpu.make_async_copy(query_rows.at[:, mine], qbuf.at[PEERS], own_sem),
        pltpu.make_async_copy(weight, wbuf.at[dp], own_sem),
    ]
    lists = [
        pltpu.make_async_copy(key_tiles_far, key_tiles, list_sem.at[0]),
        pltpu.make_async_copy(tile_counts_far, tile_counts, list_sem.at[1]),
        pltpu.make_async_copy(gate_far, gate, list_sem.at[2]),
    ]
    for copy in (*own, *lists):
        copy.start()
    pl.semaphore_wait(barrier, PEERS + 1 + 2 * (z % 2))

    @pl.when(z % 2 == 1)
    def _():
        for where in nexts:
            pl.semaphore_signal(ready, inc=1, device_id=(seq, where), device_id_type=MESH)


    def piece(p):
        return pl.ds(pl.multiple_of(p * PIECE, PIECE), PIECE)

    def hop(way, n, p, block, src=None):
        place = wbuf.at[block, piece(p)]
        return remote(place if src is None else src, place, w_send, w_recv.at[way, n], (seq, nexts[way]))

    for i in range(PEERS):
        remote(key_rows.at[:, head_columns(i)], kbuf.at[seq], k_send, k_recv, (partner(i), dp)).start()
    for i in range(PEERS):
        remote(value_rows.at[:, head_columns(i)], vbuf.at[seq], v_send, v_recv, (partner(i), dp)).start()
    for i in range(PEERS):
        remote(query_rows.at[:, head_columns(i)], qbuf.at[i], q_send, q_recv.at[i], (partner(i), dp)).start()
    remote(weight, wbuf.at[dp], c_send, c_recv, (seq, other)).start()

    @pl.when(z % 2 == 0)
    def _():
        pl.semaphore_wait(ready, 2)

    for p in range(PIECES):
        for way in range(2):
            hop(way, p, p, dp, weight.at[piece(p)]).start()

    def tick(n, swapped):
        q = n % PIECES
        for way in range(2):
            p = q + way * (PIECES // 2) * (n // (AWAY * PIECES))
            far = n // PIECES + 1
            block = ((z + RING - far) % RING if way == 0 else (z + far) % RING) * 2 + core
            hop(way, n, p, block).wait_recv()

            @pl.when((n < (AWAY - 1) * PIECES) | ((n < AWAY * PIECES) & (q // (PIECES // 2) == way)))
            def _():
                last = AWAY * PIECES + q % (PIECES // 2)
                hop(way, jnp.where(n < (AWAY - 1) * PIECES, n + PIECES, last), p, block).start()

            place = wbuf.at[block, piece(p)]
            remote(place, place, c_send, swapped, (seq, other)).start()

    for n in range(EARLY):
        tick(n, c_recv)
    bytes_of(kbuf, len(own) - 1 + HD * D // (TILE * HD), own_sem).wait()
    for copy in lists:
        copy.wait()
    bytes_of(kbuf, PEERS, k_recv).wait()
    bytes_of(vbuf, PEERS, v_recv).wait()

    orecv[seq] = attend(qbuf[PEERS], kbuf, vbuf, key_tiles, tile_counts, seq)

    def answer(i):
        a = partner(i, -1)
        return remote(obuf.at[i], orecv.at[seq], o_send, o_recv.at[seq], (a, dp))

    def step(n, carry):
        i = entry(QUERY_TURNS, n)
        a = partner(i, -1)

        @pl.when(n % 3 == 1)
        def _():
            tick(EARLY + n // 3, c_recv)

        pltpu.make_async_copy(qbuf.at[i], qbuf.at[i], q_recv.at[i]).wait()
        obuf[i] = attend(qbuf[i], kbuf, vbuf, key_tiles, tile_counts, a)
        answer(i).start()
        return carry

    lax.fori_loop(0, PEERS, step, 0)
    far = (z + RING // 2) % RING * 2
    at_a = entry(PLACES, (far // SIDE - x + SIDE) % SIDE * SIDE + (far % SIDE - y + SIDE) % SIDE)
    at_b = entry(PLACES, ((far + 1) // SIDE - x + SIDE) % SIDE * SIDE + ((far + 1) % SIDE - y + SIDE) % SIDE)
    low, high = jnp.minimum(at_a, at_b), jnp.maximum(at_a, at_b)

    def near_head(k):
        k = k + jnp.where(k >= low, 1, 0)
        k = k + jnp.where(k >= high, 1, 0)
        return (x + digit(TURN_X, k)) % SIDE * SIDE + (y + digit(TURN_Y, k)) % SIDE

    def project(heads, first=False, last=False):
        for h in heads:

            @pl.when(h != seq)
            def _():
                pltpu.make_async_copy(orecv.at[h], orecv.at[h], o_recv.at[h]).wait()

        rows = jnp.concatenate([orecv[h] for h in heads], axis=1)
        for n in range(0, D, NCHUNK):
            at = pl.ds(n, NCHUNK)
            block = jnp.concatenate([wbuf[h, :, at] for h in heads], axis=0)
            product = jnp.dot(rows, block, preferred_element_type=jnp.float32)
            if not first:
                product = acc[:, at] + product
            if last:
                out[:, at] = (gate[:, at].astype(jnp.float32) * product).astype(jnp.bfloat16)
            else:
                acc[:, at] = product

    bytes_of(wbuf, RING - 1, c_recv).wait()
    project([near_head(k) for k in range(4)], first=True)
    tick(COMING - 2, c_far)
    tick(COMING - 1, c_far)
    project([near_head(k) for k in range(4, 8)])
    bytes_of(wbuf, 1, c_far).wait()
    project([far, far + 1])
    project([near_head(k) for k in range(8, 12)])
    project([near_head(k) for k in range(12, 14)], last=True)

    bytes_of(kbuf, PEERS, k_send).wait()
    bytes_of(vbuf, PEERS, v_send).wait()
    bytes_of(qbuf, PEERS, q_send).wait()
    bytes_of(obuf, PEERS, o_send).wait()
    bytes_of(wbuf, RING - 1, w_send).wait()
    bytes_of(wbuf, RING, c_send).wait()


def shards(query_rows, key_rows, value_rows, key_tiles, tile_counts, out_weight, gate_vector):
    dma = pltpu.SemaphoreType.DMA
    far = pl.BlockSpec(memory_space=pltpu.HBM)
    near = pl.BlockSpec(memory_space=pltpu.VMEM)
    tiles = PEERS + 1
    blocks = RING * 2
    result = pl.pallas_call(
        kernel,
        name="attention_and_projection",
        out_shape=pltpu.VMEM((TILE, D), jnp.bfloat16),
        in_specs=[far] * 7,
        out_specs=near,
        scratch_shapes=[
            pltpu.SMEM((MAXK, tiles), jnp.int32),
            pltpu.SMEM((tiles,), jnp.int32),
            pltpu.VMEM((1, D), jnp.bfloat16),
            pltpu.VMEM((tiles, TILE, HD), jnp.bfloat16),
            pltpu.VMEM((tiles, TILE, HD), jnp.bfloat16),
            pltpu.VMEM((tiles, TILE, HD), jnp.bfloat16),
            pltpu.VMEM((tiles, TILE, HD), jnp.bfloat16),
            pltpu.VMEM((tiles, TILE, HD), jnp.bfloat16),
            pltpu.VMEM((blocks, HD, D), jnp.bfloat16),
            pltpu.VMEM((TILE, D), jnp.float32),
            dma, dma, dma, dma, dma, dma((PEERS,)), dma, dma((tiles,)), dma, dma((3,)),
            dma, dma((2, COMING)), dma, dma, dma, pltpu.SemaphoreType.REGULAR,
        ],
        compiler_params=pltpu.CompilerParams(
            collective_id=0, has_side_effects=True, vmem_limit_bytes=60 << 20
        ),
        cost_estimate=pl.CostEstimate(
            flops=10_000_000_000, bytes_accessed=10_000_000, transcendentals=9_000_000
        ),
    )(query_rows[0], key_rows[0], value_rows[0], key_tiles[0].T, tile_counts[0], out_weight, gate_vector)
    return result[None]


def solution(mesh):
    in_specs = (
        P("dp", "seq", None),
        P("dp", "seq", None),
        P("dp", "seq", None),
        P("dp", None, None),
        P("dp", None),
        P("dp", None),
        P("dp", None),
    )
    out_specs = P("dp", "seq", None)
    return jax.shard_map(shards, mesh=mesh, in_specs=in_specs, out_specs=out_specs, check_vma=False)
```
